32 devices in a mesh: chan: 8 (over z, y), grp: 4 (over x, core).
Axes of the slice: x: 2, y: 2, z: 4, core: 2. Of those that a mesh axis runs over, the one named last changes fastest.
Arguments:
- beam_power: bfloat16 [32, 8192, 128], P('grp', 'chan'), as said below
- trial_blocks: int32 [32], replicated, may hold values from 1 to 4, as said below
- shift_table: int32 [4, 5, 8192], replicated, may hold values from 0 to 4, as said below
Outputs:
- dm_planes: bfloat16 [32, 4, 8192, 128], P(('grp', 'chan'))
The draws below stay inside these ranges and needn't reach their ends.
Inputs may be any that keep to these rules, and one draw needn't show every extreme that they name: `beam_power`: detected power, drawn afresh for every beam, channel and sample. `trial_blocks`: DM blocks needed by each beam. `shift_table`: delays in whole tiles.
All inputs are finite; a program needn't handle non-finite values.
Results may differ from the reference program's by a relative error of at most 0.0049.
Values may be sent and summed in bfloat16 or wider, within the bound.
A program may use at most 128 MiB of HBM per device.

```python
import math
import jax
import jax.numpy as jnp
from jax import lax

NCHAN = 8192
NT = 128
SECTIONS = 5
MAXBLK = 4
TILE = 8
BEAMS = 32
MAXSH = 4


def draw_beam_power(key, part):
    key = jax.random.fold_in(key, 5)
    keys_list = jax.random.split(key, 4)
    chan_gain = jnp.exp(jax.random.uniform(keys_list[0], (NCHAN,), jnp.float32, 0.0, math.log(10.0)))
    beam_gain = jnp.exp(jax.random.uniform(keys_list[1], (BEAMS,), jnp.float32, 0.0, math.log(10.0)))
    level_base = jax.random.uniform(keys_list[2], (BEAMS, NCHAN, 1), jnp.float32, 2.0, 6.0)
    noise_part = jax.random.normal(keys_list[3], (BEAMS, NCHAN, NT), jnp.float32)
    values = beam_gain[:, None, None] * chan_gain[None, :, None] * (level_base + noise_part)
    return values.astype(jnp.bfloat16)


def draw_trial_blocks(key, part):
    key = jax.random.fold_in(key, 11)
    keys_list = jax.random.split(key, 3)
    raw_draw = jax.random.randint(keys_list[0], (BEAMS,), 0, 16)
    counts_out = 1 + (raw_draw >= 8).astype(jnp.int32) + (raw_draw >= 12).astype(jnp.int32) + (raw_draw >= 14).astype(jnp.int32)
    high_place = jax.random.randint(keys_list[1], (), 0, BEAMS)
    counts_out = counts_out.at[high_place].set(MAXBLK)
    low_place = (high_place + 1 + jax.random.randint(keys_list[2], (), 0, BEAMS - 1)) % BEAMS
    counts_out = counts_out.at[low_place].set(1)
    return counts_out.astype(jnp.int32)


def draw_shift_table(key, part):
    key = jax.random.fold_in(key, 17)
    table_out = jax.random.randint(key, (MAXBLK, SECTIONS, NCHAN), 0, MAXSH + 1)
    table_out = table_out.at[0, 0, 0].set(MAXSH)
    table_out = table_out.at[MAXBLK - 1, SECTIONS - 1, NCHAN - 1].set(0)
    return table_out.astype(jnp.int32)


def setup_inputs(seed: int = 0) -> dict:
    streams_of = jax.random.split(jax.random.key(seed), 4)
    return {
        "beam_power": draw_beam_power(jax.random.fold_in(streams_of[3], 71), 0),
        "trial_blocks": draw_trial_blocks(jax.random.fold_in(streams_of[3], 71), 0),
        "shift_table": draw_shift_table(jax.random.fold_in(streams_of[3], 71), 0),
    }


epsilon = 1e-05

def normalize(block_power):
    values = block_power.astype(jnp.float32)
    center = lax.optimization_barrier(jnp.mean(values, axis=-1, keepdims=True))
    spread = lax.optimization_barrier(jnp.mean(jnp.square(values - center), axis=-1, keepdims=True))
    return ((values - center) * lax.rsqrt(spread + epsilon)).astype(jnp.bfloat16)

def shift_tiles(block_rows, amount):
    band_count, group_size, time_len = block_rows.shape
    tile_count = time_len // TILE
    tiled = block_rows.reshape(band_count, group_size, tile_count, TILE)
    source_tile = jnp.arange(tile_count, dtype=jnp.int32)[None, None, :] - amount[:, :, None]
    picked = jnp.take_along_axis(tiled, jnp.maximum(source_tile, 0)[..., None], axis=2)
    result = jnp.where((source_tile >= 0)[..., None], picked, 0.0)
    return result.reshape(band_count, group_size, time_len)

def dedisperse(rows_in, section_shifts):
    row_count, time_len = rows_in.shape
    current = rows_in
    for level_index in range(section_shifts.shape[0]):
        half_size = 2 ** level_index
        group_size = 2 * half_size
        grouped = current.reshape(row_count // group_size, 2, half_size, time_len)
        lower_band = grouped[:, 0]
        upper_band = grouped[:, 1]
        low_rows = jnp.repeat(lower_band, 2, axis=1)
        if half_size == 1:
            high_rows = jnp.repeat(upper_band, 2, axis=1)
        else:
            high_rows = jnp.concatenate([upper_band[:, :1], jnp.repeat(upper_band[:, 1:], 2, axis=1), upper_band[:, -1:]], axis=1)
        moved_rows = shift_tiles(high_rows, section_shifts[level_index].reshape(row_count // group_size, group_size))
        current = (low_rows + moved_rows).reshape(row_count, time_len)
    return current

def reference(beam_power, trial_blocks, shift_table):
    out_scale = float(2 ** SECTIONS) ** (-0.5)

    def per_beam(inputs):
        one_power, one_count = inputs
        calibrated = normalize(one_power).astype(jnp.float32)
        planes_list = []
        for block_index in range(MAXBLK):
            time_plane = dedisperse(calibrated, shift_table[block_index]) * out_scale
            planes_list.append(jnp.where(block_index < one_count, time_plane, 0.0).astype(jnp.bfloat16))
        return jnp.stack(planes_list)
    return lax.map(per_beam, (beam_power, trial_blocks))
```

```python
import functools

import jax
import jax.numpy as jnp
from jax import lax
from jax.experimental import pallas as pl
from jax.experimental.pallas import tpu as pltpu
from jax.sharding import PartitionSpec as P

SECTIONS = 5
MAXBLK = 4
TILE = 8
BAND = 2**SECTIONS
LANES = 128

epsilon = 1e-05


def flip(me, k):
    out = me
    bit = 1
    while bit <= k:
        if k & bit:
            out = out + bit * (1 - 2 * ((me // bit) % 2))
        bit *= 2
    return out


def turn_kernel(n, bands, time_len, power_ref, recv_ref, rows, packed, send_sem, recv_sem, own_sem):
    me = lax.axis_index("chan")
    grp = lax.axis_index("grp")
    barrier = pltpu.get_barrier_semaphore()
    for k in range(1, n):
        pl.semaphore_signal(barrier, inc=1, device_id=(flip(me, k), grp), device_id_type=pl.DeviceIdType.MESH)
    pl.semaphore_wait(barrier, n - 1)

    copies = []
    for k in range(n - 1, -1, -1):
        peer = flip(me, k)
        values = power_ref[peer].astype(jnp.float32)
        center = jnp.mean(values, axis=-1, keepdims=True)
        moved = values - center
        spread = jnp.mean(jnp.square(moved), axis=-1, keepdims=True)
        rows[...] = moved * lax.rsqrt(spread + epsilon)
        for d in range(BAND):
            packed[k, d] = rows[pl.ds(d, bands, stride=BAND), :].astype(jnp.bfloat16)
        if k == 0:
            copy = pltpu.make_async_copy(packed.at[k], recv_ref.at[me], own_sem)
        else:
            copy = pltpu.make_async_remote_copy(
                src_ref=packed.at[k],
                dst_ref=recv_ref.at[me],
                send_sem=send_sem.at[k],
                recv_sem=recv_sem.at[k],
                device_id=(peer, grp),
                device_id_type=pl.DeviceIdType.MESH,
            )
        copy.start()
        copies.append(copy)
    for copy in copies:
        copy.wait()


def turn(power, n):
    beams, chans, time_len = power.shape
    bands = chans // BAND
    return pl.pallas_call(
        functools.partial(turn_kernel, n, bands, time_len),
        out_shape=jax.ShapeDtypeStruct((n, BAND, bands, time_len), jnp.bfloat16),
        in_specs=[pl.BlockSpec(memory_space=pltpu.VMEM)],
        out_specs=pl.BlockSpec(memory_space=pl.ANY),
        scratch_shapes=[
            pltpu.VMEM((chans, time_len), jnp.float32),
            pltpu.VMEM((n, BAND, bands, time_len), jnp.bfloat16),
            pltpu.SemaphoreType.DMA((n,)),
            pltpu.SemaphoreType.DMA((n,)),
            pltpu.SemaphoreType.DMA,
        ],
        compiler_params=pltpu.CompilerParams(
            collective_id=0, has_side_effects=True, vmem_limit_bytes=32 * 2**20
        ),
        name="turn",
    )(power)


def delayed(x, tiles):
    return jnp.concatenate([jnp.zeros((tiles,) + x.shape[1:], x.dtype), x[:-tiles]], axis=0)


def shift_rows(x, amount):
    one = jnp.where(((amount % 2) == 1)[None], delayed(x, 1), x)
    two = jnp.where(((amount // 2) % 2 == 1)[None], delayed(one, 2), one)
    return jnp.where((amount == 4)[None], delayed(x, 4), two)


def fdmt_kernel(n_chan, out_scale, count_ref, x_ref, tab_ref, o_ref, first, buf_a, buf_b, stage):
    block = pl.program_id(1)
    own = lax.axis_index("grp") * n_chan + lax.axis_index("chan")
    count = count_ref[own]
    sources, _, bands, time_len = x_ref.shape
    tiles = time_len // TILE

    def eye(size):
        r = lax.broadcasted_iota(jnp.int32, (size, size), 0)
        c = lax.broadcasted_iota(jnp.int32, (size, size), 1)
        return (r == c).astype(jnp.float32).astype(jnp.bfloat16)

    @pl.when(block == 0)
    def _():
        ident = eye(time_len)
        for d in range(BAND):
            if bands % 16 == 0:
                part = jnp.concatenate([x_ref[i, d] for i in range(sources)], axis=0)
            else:
                part = jnp.concatenate([x_ref[i, d].astype(jnp.float32) for i in range(sources)], axis=0)
                part = part.astype(jnp.bfloat16)
            turned = lax.dot_general(ident, part, (((1,), (1,)), ((), ())), preferred_element_type=jnp.float32)
            first[d] = turned.reshape(tiles, TILE, LANES)

    @pl.when(block < count)
    def _():
        ident = eye(LANES)
        source = first
        for s in range(SECTIONS):
            half = 2**s
            target = (buf_a, buf_b)[s % 2]
            for base in range(0, BAND, 2 * half):
                for j in range(half):
                    low = source[base + j]
                    for odd in range(2):
                        up = source[base + half + min(j + odd, half - 1)]
                        row = base + 2 * j + odd
                        amount = jnp.broadcast_to(tab_ref[0, s, pl.ds(row, 1), :], (TILE, LANES))
                        new = low + shift_rows(up, amount)
                        if s < SECTIONS - 1:
                            target[row] = new
                        else:
                            new = (new * out_scale).reshape(time_len, LANES).astype(jnp.bfloat16)
                            stage[pl.ds(row, LANES, stride=BAND), :] = lax.dot_general(
                                ident, new, (((1,), (1,)), ((), ())), preferred_element_type=jnp.float32
                            )
            source = target
        o_ref[0, 0] = stage[...].astype(jnp.bfloat16)

    @pl.when(block >= count)
    def _():
        o_ref[...] = jnp.zeros_like(o_ref)


def fdmt(counts, turned, table, n_chan):
    n, _, bands, time_len = turned.shape
    rows = n * bands * BAND
    sources = LANES // bands
    halves = n // sources
    tiles = time_len // TILE
    out_scale = float(2**SECTIONS) ** (-0.5)
    return pl.pallas_call(
        functools.partial(fdmt_kernel, n_chan, out_scale),
        grid=(halves, MAXBLK),
        out_shape=jax.ShapeDtypeStruct((1, MAXBLK, rows, time_len), jnp.bfloat16),
        in_specs=[
            pl.BlockSpec(memory_space=pltpu.SMEM),
            pl.BlockSpec((sources, BAND, bands, time_len), lambda i, j: (i, 0, 0, 0)),
            pl.BlockSpec((1, SECTIONS, BAND, LANES), lambda i, j: (j, 0, 0, i)),
        ],
        out_specs=pl.BlockSpec((1, 1, LANES * BAND, time_len), lambda i, j: (0, j, i, 0)),
        scratch_shapes=[
            pltpu.VMEM((BAND, tiles, TILE, LANES), jnp.float32),
            pltpu.VMEM((BAND, tiles, TILE, LANES), jnp.float32),
            pltpu.VMEM((BAND, tiles, TILE, LANES), jnp.float32),
            pltpu.VMEM((LANES * BAND, time_len), jnp.float32),
        ],
        compiler_params=pltpu.CompilerParams(vmem_limit_bytes=40 * 2**20),
        name="fdmt",
    )(counts, turned, table)


def body(beam_power, trial_blocks, shift_table):
    n = lax.axis_size("chan")
    blocks, sections, rows = shift_table.shape
    table = shift_table.reshape(blocks, sections, rows // BAND, BAND).swapaxes(2, 3)
    turned = turn(beam_power, n)
    return fdmt(trial_blocks, turned, table, n)


def solution(mesh):
    in_specs = (P("grp", "chan", None), P(), P())
    out_specs = P(("grp", "chan"), None, None, None)
    return jax.shard_map(body, mesh=mesh, in_specs=in_specs, out_specs=out_specs, check_vma=False)
```

```python
import functools

import jax
import jax.numpy as jnp
from jax import lax
from jax.experimental import pallas as pl
from jax.experimental.pallas import tpu as pltpu
from jax.sharding import PartitionSpec as P

SECTIONS = 5
MAXBLK = 4
TILE = 8
BAND = 2**SECTIONS
LANES = 128
MESH = pl.DeviceIdType.MESH

epsilon = 1e-05
out_scale = float(2**SECTIONS) ** (-0.5)


def flip(me, k):
    out = me
    bit = 1
    while bit <= k:
        if k & bit:
            out = out + bit * (1 - 2 * ((me // bit) % 2))
        bit *= 2
    return out


def eye(size):
    r = lax.broadcasted_iota(jnp.int32, (size, size), 0)
    c = lax.broadcasted_iota(jnp.int32, (size, size), 1)
    return (r == c).astype(jnp.float32).astype(jnp.bfloat16)


def times_transposed(a, b):
    return lax.dot_general(a, b, (((1,), (1,)), ((), ())), preferred_element_type=jnp.float32)


def bands_to_lanes(ident, x_ref, d, first):
    sources, _, bands, time_len = x_ref.shape
    if bands % 16 == 0:
        part = jnp.concatenate([x_ref[i, d] for i in range(sources)], axis=0)
    else:
        part = jnp.concatenate([x_ref[i, d].astype(jnp.float32) for i in range(sources)], axis=0)
        part = part.astype(jnp.bfloat16)
    first[d] = times_transposed(ident, part).reshape(time_len // TILE, TILE, LANES)


def merge_row(source, low_row, up_row, amount):
    tiles = source.shape[1]
    odd = (amount == 1) | (amount == 3)
    two = (amount == 2) | (amount == 3)
    four = amount == 4
    zero = jnp.zeros((TILE, LANES), jnp.float32)
    ups, ones, out = [], [], []
    for t in range(tiles):
        ups.append(source[up_row, t])
        ones.append(jnp.where(odd, ups[t - 1] if t >= 1 else zero, ups[t]))
        value = jnp.where(two, ones[t - 2] if t >= 2 else zero, ones[t])
        value = jnp.where(four, ups[t - 4] if t >= 4 else zero, value)
        out.append(source[low_row, t] + value)
    return out


def merge_pair(s, p, source, target, table_row, ident, stage):
    half = 2**s
    base = (p // half) * (2 * half)
    j = p % half
    if isinstance(p, int):
        after = min(j + 1, half - 1)
    else:
        after = jnp.minimum(j + 1, half - 1)
    rows = []
    for odd, up in ((0, j), (1, after)):
        amount = jnp.broadcast_to(table_row(s, 2 * p + odd), (TILE, LANES))
        rows.append(merge_row(source, base + j, base + half + up, amount))
    if s < SECTIONS - 1:
        for odd in range(2):
            for t, value in enumerate(rows[odd]):
                target[2 * p + odd, t] = value
        return
    time_len = len(rows[0]) * TILE
    both = [(value * out_scale) for row in rows for value in row]
    both = jnp.concatenate(both, axis=0).astype(jnp.bfloat16)
    turned = times_transposed(ident, both)
    for odd in range(2):
        stage[pl.ds(2 * p + odd, LANES, stride=BAND), :] = turned[:, odd * time_len : (odd + 1) * time_len]


def turn_kernel(
    n, bands, time_len,
    power_hbm, table_hbm,
    near_out, far_ref, far_table,
    power, table, rows, packed, near, lines, tab_near, tab_far, first, buf_a, buf_b, stage, planes,
    in_sem, table_sem, send_sem, recv_sem, own_sem, out_sem, tab_sem,
):
    me = lax.axis_index("chan")
    grp = lax.axis_index("grp")
    middle = n // 2
    order = []
    for i in range(middle):
        order += [n - 1 - i, middle - 1 - i]

    loads = {}
    for k in order:
        loads[k] = pltpu.make_async_copy(power_hbm.at[flip(me, k)], power.at[k], in_sem.at[k])
        loads[k].start()
    table_load = pltpu.make_async_copy(table_hbm, table, table_sem)
    table_load.start()

    barrier = pltpu.get_barrier_semaphore()
    for k in range(1, n):
        pl.semaphore_signal(barrier, inc=1, device_id=(flip(me, k), grp), device_id_type=MESH)
    pl.semaphore_wait(barrier, n - 1)

    copies = {}
    slot = me % middle
    for k in order:
        loads[k].wait()
        values = power[k].astype(jnp.float32)
        center = jnp.mean(values, axis=-1, keepdims=True)
        moved = values - center
        spread = jnp.mean(jnp.square(moved), axis=-1, keepdims=True)
        rows[...] = moved * lax.rsqrt(spread + epsilon)
        for d in range(BAND):
            packed[k, d] = rows[pl.ds(d, bands, stride=BAND), :].astype(jnp.bfloat16)
        if k == 0:
            copies[k] = pltpu.make_async_copy(packed.at[k], near.at[slot], own_sem)
        else:
            copies[k] = pltpu.make_async_remote_copy(
                src_ref=packed.at[k],
                dst_ref=(near if k < middle else far_ref).at[slot],
                send_sem=send_sem.at[k],
                recv_sem=recv_sem.at[k],
                device_id=(flip(me, k), grp),
                device_id_type=MESH,
            )
        copies[k].start()

    table_load.wait()
    ident = eye(LANES)
    groups = table.shape[2] // LANES
    per_group = LANES // BAND
    group_row = lax.broadcasted_iota(jnp.int32, (groups, LANES), 0)
    lane = lax.broadcasted_iota(jnp.int32, (groups, LANES), 1)
    near_half = me // middle

    def order_table(s, carry):
        for c in range(groups):
            lines[pl.ds(c, MAXBLK, stride=groups), :] = table[s, :, c * LANES : (c + 1) * LANES].astype(
                jnp.float32
            )
        for block in range(MAXBLK):
            part = lines[block * groups : (block + 1) * groups, :].astype(jnp.bfloat16)
            turned = times_transposed(ident, part).astype(jnp.bfloat16)
            for half, target in ((near_half, tab_near), (1 - near_half, tab_far)):
                total = jnp.zeros((BAND, LANES), jnp.float32)
                for b in range(per_group):
                    place = (group_row * per_group + b) - half * LANES == lane
                    place = place.astype(jnp.float32).astype(jnp.bfloat16)
                    total += jnp.dot(
                        turned[b * BAND : (b + 1) * BAND], place, preferred_element_type=jnp.float32
                    )
                target[block, s] = total.astype(jnp.int32)
        return carry

    lax.fori_loop(0, SECTIONS, order_table, 0)
    tab_copy = pltpu.make_async_copy(tab_far, far_table, tab_sem)
    tab_copy.start()

    for k in range(middle):
        if k == 0:
            copies[k].wait()
        else:
            copies[k].wait_recv()

    def fill(d, carry):
        bands_to_lanes(ident, near, d, first)
        return carry

    lax.fori_loop(0, BAND, fill, 0)

    def near_block(block, carry):
        def table_row(s, row):
            return tab_near[block, s, pl.ds(row, 1), :]

        source = first
        for s in range(SECTIONS):
            target = (buf_a, buf_b)[s % 2]

            def step(p, inner, s=s, source=source, target=target):
                merge_pair(s, p, source, target, table_row, ident, stage)
                return inner

            lax.fori_loop(0, BAND // 2, step, 0)
            source = target
        planes[block] = stage[...].astype(jnp.bfloat16)
        pltpu.make_async_copy(planes.at[block], near_out.at[block], out_sem.at[block]).start()
        return carry

    lax.fori_loop(0, MAXBLK, near_block, 0)

    for k in range(1, n):
        copies[k].wait_send()
    for k in range(middle, n):
        copies[k].wait_recv()
    for block in range(MAXBLK):
        pltpu.make_async_copy(planes.at[block], near_out.at[block], out_sem.at[block]).wait()
    tab_copy.wait()


def turn(power, table, n):
    beams, chans, time_len = power.shape
    bands = chans // BAND
    sections, blocks, total_rows = table.shape
    half_rows = LANES * BAND
    tiles = time_len // TILE
    groups = total_rows // LANES
    any_spec = pl.BlockSpec(memory_space=pl.ANY)
    wide = pltpu.VMEM((BAND, tiles, TILE, LANES), jnp.float32)
    ordered = (blocks, sections, BAND, LANES)
    return pl.pallas_call(
        functools.partial(turn_kernel, n, bands, time_len),
        out_shape=(
            jax.ShapeDtypeStruct((blocks, half_rows, time_len), jnp.bfloat16),
            jax.ShapeDtypeStruct((n // 2, BAND, bands, time_len), jnp.bfloat16),
            jax.ShapeDtypeStruct(ordered, jnp.int32),
        ),
        in_specs=[any_spec, any_spec],
        out_specs=(any_spec, any_spec, any_spec),
        scratch_shapes=[
            pltpu.VMEM((n, chans, time_len), jnp.bfloat16),
            pltpu.VMEM(table.shape, jnp.int32),
            pltpu.VMEM((chans, time_len), jnp.float32),
            pltpu.VMEM((n, BAND, bands, time_len), jnp.bfloat16),
            pltpu.VMEM((n // 2, BAND, bands, time_len), jnp.bfloat16),
            pltpu.VMEM((blocks * groups, LANES), jnp.float32),
            pltpu.VMEM(ordered, jnp.int32),
            pltpu.VMEM(ordered, jnp.int32),
            wide,
            wide,
            wide,
            pltpu.VMEM((half_rows, time_len), jnp.float32),
            pltpu.VMEM((blocks, half_rows, time_len), jnp.bfloat16),
            pltpu.SemaphoreType.DMA((n,)),
            pltpu.SemaphoreType.DMA,
            pltpu.SemaphoreType.DMA((n,)),
            pltpu.SemaphoreType.DMA((n,)),
            pltpu.SemaphoreType.DMA,
            pltpu.SemaphoreType.DMA((blocks,)),
            pltpu.SemaphoreType.DMA,
        ],
        compiler_params=pltpu.CompilerParams(
            collective_id=0, has_side_effects=True, vmem_limit_bytes=58 * 2**20
        ),
        name="turn",
    )(power, table)


def fdmt_kernel(n, count_ref, x_ref, tab_ref, near_ref, o_ref, first, buf_a, buf_b, stage):
    block = pl.program_id(0)
    me = lax.axis_index("chan")
    count = count_ref[lax.axis_index("grp") * n + me]
    near_half = me // (n // 2)
    half_rows = near_ref.shape[1]

    def rows_of(half):
        return pl.ds(pl.multiple_of(half * half_rows, half_rows), half_rows)

    @pl.when(block == 0)
    def _():
        ident = eye(x_ref.shape[3])
        for d in range(BAND):
            bands_to_lanes(ident, x_ref, d, first)

    @pl.when(block < count)
    def _():
        ident = eye(LANES)

        def table_row(s, row):
            return tab_ref[0, s, pl.ds(row, 1), :]

        source = first
        for s in range(SECTIONS):
            target = (buf_a, buf_b)[s % 2]
            for p in range(BAND // 2):
                merge_pair(s, p, source, target, table_row, ident, stage)
            source = target
        o_ref[0, 0, rows_of(near_half), :] = near_ref[0]
        o_ref[0, 0, rows_of(1 - near_half), :] = stage[...].astype(jnp.bfloat16)

    @pl.when(block >= count)
    def _():
        o_ref[...] = jnp.zeros_like(o_ref)


def fdmt(counts, far, table, near, n):
    sources, _, bands, time_len = far.shape
    blocks, half_rows, _ = near.shape
    rows = 2 * half_rows
    wide = pltpu.VMEM((BAND, time_len // TILE, TILE, LANES), jnp.float32)
    return pl.pallas_call(
        functools.partial(fdmt_kernel, n),
        grid=(blocks,),
        out_shape=jax.ShapeDtypeStruct((1, blocks, rows, time_len), jnp.bfloat16),
        in_specs=[
            pl.BlockSpec(memory_space=pltpu.SMEM),
            pl.BlockSpec(far.shape, lambda j: (0, 0, 0, 0)),
            pl.BlockSpec((1,) + table.shape[1:], lambda j: (j, 0, 0, 0)),
            pl.BlockSpec((1, half_rows, time_len), lambda j: (j, 0, 0)),
        ],
        out_specs=pl.BlockSpec((1, 1, rows, time_len), lambda j: (0, j, 0, 0)),
        scratch_shapes=[wide, wide, wide, pltpu.VMEM((half_rows, time_len), jnp.float32)],
        compiler_params=pltpu.CompilerParams(vmem_limit_bytes=58 * 2**20),
        name="fdmt",
    )(counts, far, table, near)


def body(beam_power, trial_blocks, shift_table):
    n = lax.axis_size("chan")
    near, far, far_table = turn(beam_power, shift_table.swapaxes(0, 1), n)
    return fdmt(trial_blocks, far, far_table, near, n)


def solution(mesh):
    in_specs = (P("grp", "chan", None), P(), P())
    out_specs = P(("grp", "chan"), None, None, None)
    return jax.shard_map(body, mesh=mesh, in_specs=in_specs, out_specs=out_specs, check_vma=False)
```

```python
import functools

import jax
import jax.numpy as jnp
from jax import lax
from jax.experimental import pallas as pl
from jax.experimental.pallas import tpu as pltpu
from jax.sharding import PartitionSpec as P

SECTIONS = 5
MAXBLK = 4
TILE = 8
BAND = 2**SECTIONS
LANES = 128
MESH = pl.DeviceIdType.MESH

epsilon = 1e-05
out_scale = float(2**SECTIONS) ** (-0.5)


def flip(me, k):
    out = me
    bit = 1
    while bit <= k:
        if k & bit:
            out = out + bit * (1 - 2 * ((me // bit) % 2))
        bit *= 2
    return out


def eye(size):
    r = lax.broadcasted_iota(jnp.int32, (size, size), 0)
    c = lax.broadcasted_iota(jnp.int32, (size, size), 1)
    return (r == c).astype(jnp.float32).astype(jnp.bfloat16)


def times_transposed(a, b):
    return lax.dot_general(a, b, (((1,), (1,)), ((), ())), preferred_element_type=jnp.float32)


def bands_to_lanes(ident, x_ref, d, first):
    sources, _, bands, time_len = x_ref.shape
    if bands % 16 == 0:
        part = jnp.concatenate([x_ref[i, d] for i in range(sources)], axis=0)
    else:
        part = jnp.concatenate([x_ref[i, d].astype(jnp.float32) for i in range(sources)], axis=0)
        part = part.astype(jnp.bfloat16)
    turned = times_transposed(ident, part)
    if sources * bands < LANES:
        turned = jnp.concatenate([turned[: time_len // 2], turned[time_len // 2 :]], axis=1)
    first[d] = turned.reshape(first.shape[1:])


def merge_row(source, low_row, up_row, amount, split):
    tiles = source.shape[1]
    odd = (amount == 1) | (amount == 3)
    two = (amount == 2) | (amount == 3)
    four = amount == 4
    zero = jnp.zeros((TILE, LANES), jnp.float32)
    ups = {t: source[up_row, t] for t in range(tiles)}
    if split:
        late = lax.broadcasted_iota(jnp.int32, (TILE, LANES), 1) >= LANES // 2
        for t in range(-4, 0):
            ups[t] = jnp.where(late, pltpu.roll(ups[tiles + t], LANES // 2, 1), zero)
    ones, out = {}, []
    for t in range(-2 if split else 0, tiles):
        ones[t] = jnp.where(odd, ups.get(t - 1, zero), ups[t])
    for t in range(tiles):
        value = jnp.where(two, ones.get(t - 2, zero), ones[t])
        value = jnp.where(four, ups.get(t - 4, zero), value)
        out.append(source[low_row, t] + value)
    return out


def merge_pair(s, p, source, target, table_row, ident, stage, split):
    half = 2**s
    base = (p // half) * (2 * half)
    j = p % half
    if isinstance(p, int):
        after = min(j + 1, half - 1)
    else:
        after = jnp.minimum(j + 1, half - 1)
    rows = []
    for odd, up in ((0, j), (1, after)):
        amount = jnp.broadcast_to(table_row(s, 2 * p + odd), (TILE, LANES))
        rows.append(merge_row(source, base + j, base + half + up, amount, split))
    if s < SECTIONS - 1:
        for odd in range(2):
            for t, value in enumerate(rows[odd]):
                target[2 * p + odd, t] = value
        return
    time_len = len(rows[0]) * TILE
    both = [(value * out_scale) for row in rows for value in row]
    both = jnp.concatenate(both, axis=0).astype(jnp.bfloat16)
    turned = times_transposed(ident, both)
    bands = LANES // 2 if split else LANES
    for odd in range(2):
        row = turned[:, odd * time_len : (odd + 1) * time_len]
        if split:
            row = jnp.concatenate([row[:bands], row[bands:]], axis=1)
        stage[pl.ds(2 * p + odd, bands, stride=BAND), :] = row


def sections_loop(first, buf_a, buf_b, stage, table_row, ident, split):
    source = first
    for s in range(SECTIONS):
        target = (buf_a, buf_b)[s % 2]

        def step(p, inner, s=s, source=source, target=target):
            merge_pair(s, p, source, target, table_row, ident, stage, split)
            return inner

        lax.fori_loop(0, BAND // 2, step, 0)
        source = target


def turn_kernel(
    n, bands, time_len,
    power_hbm, table_hbm,
    near_out, mid_out, far_ref, far_table,
    power, table, rows, packed, near, mid, lines, tab_near, tab_mid, tab_far,
    first, buf_a, buf_b, stage, first_q, buf_aq, buf_bq, stage_q, planes, planes_q,
    in_sem, table_sem, send_sem, recv_sem, own_sem, out_sem, out_sem_q, tab_sem,
):
    me = lax.axis_index("chan")
    grp = lax.axis_index("grp")
    half = n // 2
    quarter = n // 4
    order = list(range(half, half + quarter)) + list(range(half - 1, -1, -1)) + list(range(half + quarter, n))

    loads = {}
    for k in order:
        loads[k] = pltpu.make_async_copy(power_hbm.at[flip(me, k)], power.at[k], in_sem.at[k])
        loads[k].start()
    table_load = pltpu.make_async_copy(table_hbm, table, table_sem)
    table_load.start()

    barrier = pltpu.get_barrier_semaphore()
    for k in range(1, n):
        pl.semaphore_signal(barrier, inc=1, device_id=(flip(me, k), grp), device_id_type=MESH)
    pl.semaphore_wait(barrier, n - 1)

    copies = {}
    for k in order:
        loads[k].wait()
        values = power[k].astype(jnp.float32)
        center = jnp.mean(values, axis=-1, keepdims=True)
        moved = values - center
        spread = jnp.mean(jnp.square(moved), axis=-1, keepdims=True)
        rows[...] = moved * lax.rsqrt(spread + epsilon)
        for d in range(BAND):
            packed[k, d] = rows[pl.ds(d, bands, stride=BAND), :].astype(jnp.bfloat16)
        if k < half:
            place = near.at[me % half]
        elif k < half + quarter:
            place = mid.at[me % quarter]
        else:
            place = far_ref.at[me % quarter]
        if k == 0:
            copies[k] = pltpu.make_async_copy(packed.at[k], place, own_sem)
        else:
            copies[k] = pltpu.make_async_remote_copy(
                src_ref=packed.at[k],
                dst_ref=place,
                send_sem=send_sem.at[k],
                recv_sem=recv_sem.at[k],
                device_id=(flip(me, k), grp),
                device_id_type=MESH,
            )
        copies[k].start()

    table_load.wait()
    ident = eye(LANES)
    groups = table.shape[2] // LANES
    per_group = LANES // BAND
    group_row = lax.broadcasted_iota(jnp.int32, (groups, LANES), 0)
    lane = lax.broadcasted_iota(jnp.int32, (groups, LANES), 1)
    lane_q = lane % (LANES // 2)
    parts = (
        ((me // half) * LANES, lane, tab_near),
        ((flip(me, half) // quarter) * (LANES // 2), lane_q, tab_mid),
        ((flip(me, half + quarter) // quarter) * (LANES // 2), lane_q, tab_far),
    )

    def order_table(s, carry):
        for c in range(groups):
            lines[pl.ds(c, MAXBLK, stride=groups), :] = table[s, :, c * LANES : (c + 1) * LANES].astype(
                jnp.float32
            )
        for block in range(MAXBLK):
            part = lines[block * groups : (block + 1) * groups, :].astype(jnp.bfloat16)
            turned = times_transposed(ident, part).astype(jnp.bfloat16)
            for start, lanes, target in parts:
                total = jnp.zeros((BAND, LANES), jnp.float32)
                for b in range(per_group):
                    place = (group_row * per_group + b) - start == lanes
                    place = place.astype(jnp.float32).astype(jnp.bfloat16)
                    total += jnp.dot(
                        turned[b * BAND : (b + 1) * BAND], place, preferred_element_type=jnp.float32
                    )
                target[block, s] = total.astype(jnp.int32)
        return carry

    lax.fori_loop(0, SECTIONS, order_table, 0)
    tab_copy = pltpu.make_async_copy(tab_far, far_table, tab_sem)
    tab_copy.start()

    copies[0].wait()
    for k in range(1, half):
        copies[k].wait_recv()

    def fill(d, carry):
        bands_to_lanes(ident, near, d, first)
        return carry

    lax.fori_loop(0, BAND, fill, 0)

    def near_block(block, carry):
        def table_row(s, row):
            return tab_near[block, s, pl.ds(row, 1), :]

        sections_loop(first, buf_a, buf_b, stage, table_row, ident, False)
        planes[block] = stage[...].astype(jnp.bfloat16)
        pltpu.make_async_copy(planes.at[block], near_out.at[block], out_sem.at[block]).start()
        return carry

    lax.fori_loop(0, MAXBLK, near_block, 0)

    for k in range(half, half + quarter):
        copies[k].wait_recv()

    def fill_q(d, carry):
        bands_to_lanes(ident, mid, d, first_q)
        return carry

    lax.fori_loop(0, BAND, fill_q, 0)

    def mid_block(block, carry):
        def table_row(s, row):
            return tab_mid[block, s, pl.ds(row, 1), :]

        sections_loop(first_q, buf_aq, buf_bq, stage_q, table_row, ident, True)
        planes_q[block] = stage_q[...].astype(jnp.bfloat16)
        pltpu.make_async_copy(planes_q.at[block], mid_out.at[block], out_sem_q.at[block]).start()
        return carry

    lax.fori_loop(0, MAXBLK, mid_block, 0)

    for block in range(MAXBLK):
        pltpu.make_async_copy(planes.at[block], near_out.at[block], out_sem.at[block]).wait()
        pltpu.make_async_copy(planes_q.at[block], mid_out.at[block], out_sem_q.at[block]).wait()
    tab_copy.wait()
    for k in range(1, n):
        copies[k].wait_send()
    for k in range(half + quarter, n):
        copies[k].wait_recv()


def turn(power, table, n):
    beams, chans, time_len = power.shape
    bands = chans // BAND
    sections, blocks, total_rows = table.shape
    half_rows = LANES * BAND
    tiles = time_len // TILE
    groups = total_rows // LANES
    any_spec = pl.BlockSpec(memory_space=pl.ANY)
    wide = pltpu.VMEM((BAND, tiles, TILE, LANES), jnp.float32)
    wide_q = pltpu.VMEM((BAND, tiles // 2, TILE, LANES), jnp.float32)
    ordered = (blocks, sections, BAND, LANES)
    return pl.pallas_call(
        functools.partial(turn_kernel, n, bands, time_len),
        out_shape=(
            jax.ShapeDtypeStruct((blocks, half_rows, time_len), jnp.bfloat16),
            jax.ShapeDtypeStruct((blocks, half_rows // 2, time_len), jnp.bfloat16),
            jax.ShapeDtypeStruct((n // 4, BAND, bands, time_len), jnp.bfloat16),
            jax.ShapeDtypeStruct(ordered, jnp.int32),
        ),
        in_specs=[any_spec, any_spec],
        out_specs=(any_spec, any_spec, any_spec, any_spec),
        scratch_shapes=[
            pltpu.VMEM((n, chans, time_len), jnp.bfloat16),
            pltpu.VMEM(table.shape, jnp.int32),
            pltpu.VMEM((chans, time_len), jnp.float32),
            pltpu.VMEM((n, BAND, bands, time_len), jnp.bfloat16),
            pltpu.VMEM((n // 2, BAND, bands, time_len), jnp.bfloat16),
            pltpu.VMEM((n // 4, BAND, bands, time_len), jnp.bfloat16),
            pltpu.VMEM((blocks * groups, LANES), jnp.float32),
            pltpu.VMEM(ordered, jnp.int32),
            pltpu.VMEM(ordered, jnp.int32),
            pltpu.VMEM(ordered, jnp.int32),
            wide,
            wide,
            wide,
            pltpu.VMEM((half_rows, time_len), jnp.float32),
            wide_q,
            wide_q,
            wide_q,
            pltpu.VMEM((half_rows // 2, time_len), jnp.float32),
            pltpu.VMEM((blocks, half_rows, time_len), jnp.bfloat16),
            pltpu.VMEM((blocks, half_rows // 2, time_len), jnp.bfloat16),
            pltpu.SemaphoreType.DMA((n,)),
            pltpu.SemaphoreType.DMA,
            pltpu.SemaphoreType.DMA((n,)),
            pltpu.SemaphoreType.DMA((n,)),
            pltpu.SemaphoreType.DMA,
            pltpu.SemaphoreType.DMA((blocks,)),
            pltpu.SemaphoreType.DMA((blocks,)),
            pltpu.SemaphoreType.DMA,
        ],
        compiler_params=pltpu.CompilerParams(
            collective_id=0, has_side_effects=True, vmem_limit_bytes=58 * 2**20
        ),
        name="turn",
    )(power, table)


def fdmt_kernel(n, count_ref, x_ref, tab_ref, near_ref, mid_ref, o_ref, first, buf_a, buf_b, stage):
    block = pl.program_id(0)
    me = lax.axis_index("chan")
    count = count_ref[lax.axis_index("grp") * n + me]
    half = n // 2
    quarter = n // 4
    quarter_rows = mid_ref.shape[1]

    def rows_of(first_quarter, size):
        start = pl.multiple_of(first_quarter * quarter_rows, quarter_rows)
        return pl.ds(start, size * quarter_rows)

    @pl.when(block == 0)
    def _():
        ident = eye(x_ref.shape[3])
        for d in range(BAND):
            bands_to_lanes(ident, x_ref, d, first)

    @pl.when(block < count)
    def _():
        ident = eye(LANES)

        def table_row(s, row):
            return tab_ref[0, s, pl.ds(row, 1), :]

        o_ref[0, 0, rows_of((me // half) * 2, 2), :] = near_ref[0]
        o_ref[0, 0, rows_of(flip(me, half) // quarter, 1), :] = mid_ref[0]
        source = first
        for s in range(SECTIONS):
            target = (buf_a, buf_b)[s % 2]
            for p in range(BAND // 2):
                merge_pair(s, p, source, target, table_row, ident, stage, True)
            source = target
        o_ref[0, 0, rows_of(flip(me, half + quarter) // quarter, 1), :] = stage[...].astype(jnp.bfloat16)

    @pl.when(block >= count)
    def _():
        o_ref[...] = jnp.zeros_like(o_ref)


def fdmt(counts, far, table, near, mid, n):
    sources, _, bands, time_len = far.shape
    blocks, half_rows, _ = near.shape
    rows = 2 * half_rows
    wide = pltpu.VMEM((BAND, time_len // TILE // 2, TILE, LANES), jnp.float32)
    return pl.pallas_call(
        functools.partial(fdmt_kernel, n),
        grid=(blocks,),
        out_shape=jax.ShapeDtypeStruct((1, blocks, rows, time_len), jnp.bfloat16),
        in_specs=[
            pl.BlockSpec(memory_space=pltpu.SMEM),
            pl.BlockSpec(far.shape, lambda j: (0, 0, 0, 0)),
            pl.BlockSpec((1,) + table.shape[1:], lambda j: (j, 0, 0, 0)),
            pl.BlockSpec((1, half_rows, time_len), lambda j: (j, 0, 0)),
            pl.BlockSpec((1, half_rows // 2, time_len), lambda j: (j, 0, 0)),
        ],
        out_specs=pl.BlockSpec((1, 1, rows, time_len), lambda j: (0, j, 0, 0)),
        scratch_shapes=[wide, wide, wide, pltpu.VMEM((half_rows // 2, time_len), jnp.float32)],
        compiler_params=pltpu.CompilerParams(vmem_limit_bytes=58 * 2**20),
        name="fdmt",
    )(counts, far, table, near, mid)


def body(beam_power, trial_blocks, shift_table):
    n = lax.axis_size("chan")
    near, mid, far, far_table = turn(beam_power, shift_table.swapaxes(0, 1), n)
    return fdmt(trial_blocks, far, far_table, near, mid, n)


def solution(mesh):
    in_specs = (P("grp", "chan", None), P(), P())
    out_specs = P(("grp", "chan"), None, None, None)
    return jax.shard_map(body, mesh=mesh, in_specs=in_specs, out_specs=out_specs, check_vma=False)
```

```python
import functools

import jax
import jax.numpy as jnp
from jax import lax
from jax.experimental import pallas as pl
from jax.experimental.pallas import tpu as pltpu
from jax.sharding import PartitionSpec as P

SECTIONS = 5
MAXBLK = 4
TILE = 8
BAND = 2**SECTIONS
LANES = 128
AT_ONCE = 4
MESH = pl.DeviceIdType.MESH

epsilon = 1e-05
out_scale = float(2**SECTIONS) ** (-0.5)


def flip(me, k):
    out = me
    bit = 1
    while bit <= k:
        if k & bit:
            out = out + bit * (1 - 2 * ((me // bit) % 2))
        bit *= 2
    return out


def eye(size):
    r = lax.broadcasted_iota(jnp.int32, (size, size), 0)
    c = lax.broadcasted_iota(jnp.int32, (size, size), 1)
    return (r == c).astype(jnp.float32).astype(jnp.bfloat16)


def times_transposed(a, b):
    return lax.dot_general(a, b, (((1,), (1,)), ((), ())), preferred_element_type=jnp.float32)


def bands_to_lanes(ident, x_ref, d, first):
    sources, _, bands, time_len = x_ref.shape
    if bands % 16 == 0:
        part = jnp.concatenate([x_ref[i, d] for i in range(sources)], axis=0)
    else:
        part = jnp.concatenate([x_ref[i, d].astype(jnp.float32) for i in range(sources)], axis=0)
        part = part.astype(jnp.bfloat16)
    turned = times_transposed(ident, part)
    if sources * bands < LANES:
        turned = jnp.concatenate([turned[: time_len // 2], turned[time_len // 2 :]], axis=1)
    first[d] = turned.reshape(first.shape[1:])


def merge_row(source, low_row, up_row, amount, split):
    tiles = source.shape[1]
    odd = (amount == 1) | (amount == 3)
    two = (amount == 2) | (amount == 3)
    four = amount == 4
    zero = jnp.zeros((TILE, LANES), jnp.float32)
    ups = {t: source[up_row, t] for t in range(tiles)}
    if split:
        late = lax.broadcasted_iota(jnp.int32, (TILE, LANES), 1) >= LANES // 2
        for t in range(-4, 0):
            ups[t] = jnp.where(late, pltpu.roll(ups[tiles + t], LANES // 2, 1), zero)
    ones, out = {}, []
    for t in range(-2 if split else 0, tiles):
        ones[t] = jnp.where(odd, ups.get(t - 1, zero), ups[t])
    for t in range(tiles):
        value = jnp.where(two, ones.get(t - 2, zero), ones[t])
        value = jnp.where(four, ups.get(t - 4, zero), value)
        out.append(source[low_row, t] + value)
    return out


def merge_pair(s, p, source, target, table_row, ident, stage, split):
    half = 2**s
    base = (p // half) * (2 * half)
    j = p % half
    if isinstance(p, int):
        after = min(j + 1, half - 1)
    else:
        after = jnp.minimum(j + 1, half - 1)
    rows = []
    for odd, up in ((0, j), (1, after)):
        amount = jnp.broadcast_to(table_row(s, 2 * p + odd), (TILE, LANES))
        rows.append(merge_row(source, base + j, base + half + up, amount, split))
    if s < SECTIONS - 1:
        for odd in range(2):
            for t, value in enumerate(rows[odd]):
                target[2 * p + odd, t] = value
        return
    time_len = len(rows[0]) * TILE
    both = [(value * out_scale) for row in rows for value in row]
    both = jnp.concatenate(both, axis=0).astype(jnp.bfloat16)
    turned = times_transposed(ident, both)
    bands = LANES // 2 if split else LANES
    for odd in range(2):
        row = turned[:, odd * time_len : (odd + 1) * time_len]
        if split:
            row = jnp.concatenate([row[:bands], row[bands:]], axis=1)
        stage[pl.ds(2 * p + odd, bands, stride=BAND), :] = row


def sections_loop(first, buf_a, buf_b, stage, table_row, ident, split):
    source = first
    for s in range(SECTIONS):
        target = (buf_a, buf_b)[s % 2]

        def step(i, inner, s=s, source=source, target=target):
            for p in range(AT_ONCE):
                merge_pair(s, i * AT_ONCE + p, source, target, table_row, ident, stage, split)
            return inner

        lax.fori_loop(0, BAND // 2 // AT_ONCE, step, 0)
        source = target


def turn_kernel(
    n, bands, time_len,
    power_hbm, table_hbm,
    near_out, mid_out, far_ref, far_table,
    power, table, rows, packed, near, mid, lines, tab_near, tab_mid, tab_far,
    first, buf_a, buf_b, stage, first_q, buf_aq, buf_bq, stage_q, planes, planes_q,
    in_sem, table_sem, send_sem, recv_sem, own_sem, out_sem, out_sem_q, tab_sem,
):
    me = lax.axis_index("chan")
    grp = lax.axis_index("grp")
    half = n // 2
    quarter = n // 4
    order = list(range(half, half + quarter)) + list(range(half - 1, -1, -1)) + list(range(half + quarter, n))

    loads = {}
    for k in order:
        loads[k] = pltpu.make_async_copy(power_hbm.at[flip(me, k)], power.at[k], in_sem.at[k])
        loads[k].start()
    table_load = pltpu.make_async_copy(table_hbm, table, table_sem)
    table_load.start()

    barrier = pltpu.get_barrier_semaphore()
    for k in range(1, n):
        pl.semaphore_signal(barrier, inc=1, device_id=(flip(me, k), grp), device_id_type=MESH)
    pl.semaphore_wait(barrier, n - 1)

    copies = {}
    for k in order:
        loads[k].wait()
        values = power[k].astype(jnp.float32)
        center = jnp.mean(values, axis=-1, keepdims=True)
        moved = values - center
        spread = jnp.mean(jnp.square(moved), axis=-1, keepdims=True)
        rows[...] = moved * lax.rsqrt(spread + epsilon)
        for d in range(BAND):
            packed[k, d] = rows[pl.ds(d, bands, stride=BAND), :].astype(jnp.bfloat16)
        if k < half:
            place = near.at[me % half]
        elif k < half + quarter:
            place = mid.at[me % quarter]
        else:
            place = far_ref.at[me % quarter]
        if k == 0:
            copies[k] = pltpu.make_async_copy(packed.at[k], place, own_sem)
        else:
            copies[k] = pltpu.make_async_remote_copy(
                src_ref=packed.at[k],
                dst_ref=place,
                send_sem=send_sem.at[k],
                recv_sem=recv_sem.at[k],
                device_id=(flip(me, k), grp),
                device_id_type=MESH,
            )
        copies[k].start()

    table_load.wait()
    ident = eye(LANES)
    groups = table.shape[2] // LANES
    per_group = LANES // BAND
    pairs = SECTIONS * MAXBLK // 2

    def spread_table(s, carry):
        for c in range(groups):
            lines[pl.ds(s * (MAXBLK * groups) + c, MAXBLK, stride=groups), :] = table[
                s, :, c * LANES : (c + 1) * LANES
            ].astype(jnp.float32)
        return carry

    lax.fori_loop(0, SECTIONS, spread_table, 0)
    turned = times_transposed(ident, lines[...].astype(jnp.bfloat16))
    turned = jnp.concatenate(
        [
            jnp.concatenate(
                [
                    turned[b * BAND : (b + 1) * BAND, q * 2 * groups : (q + 1) * 2 * groups]
                    for b in range(per_group)
                ],
                axis=1,
            )
            for q in range(pairs)
        ],
        axis=0,
    ).astype(jnp.bfloat16)
    shape = (per_group * 2 * groups, 2 * LANES)
    index = lax.broadcasted_iota(jnp.int32, shape, 0)
    lane = lax.broadcasted_iota(jnp.int32, shape, 1)
    same = (index // groups) % 2 == lane // LANES
    band = (index % groups) * per_group + index // (2 * groups)
    parts = (
        ((me // half) * LANES, lane % LANES, tab_near),
        ((flip(me, half) // quarter) * (LANES // 2), lane % (LANES // 2), tab_mid),
        ((flip(me, half + quarter) // quarter) * (LANES // 2), lane % (LANES // 2), tab_far),
    )
    for start, lanes, target in parts:
        place = (same & (band - start == lanes)).astype(jnp.float32).astype(jnp.bfloat16)
        placed = jnp.dot(turned, place, preferred_element_type=jnp.float32).astype(jnp.int32)
        for q in range(pairs):
            for i in range(2):
                s, block = divmod(2 * q + i, MAXBLK)
                target[block, s] = placed[q * BAND : (q + 1) * BAND, i * LANES : (i + 1) * LANES]
    tab_copy = pltpu.make_async_copy(tab_far, far_table, tab_sem)
    tab_copy.start()

    copies[0].wait()
    for k in range(1, half):
        copies[k].wait_recv()

    for d in range(BAND):
        bands_to_lanes(ident, near, d, first)

    def near_block(block, carry):
        def table_row(s, row):
            return tab_near[block, s, pl.ds(row, 1), :]

        sections_loop(first, buf_a, buf_b, stage, table_row, ident, False)
        planes[block] = stage[...].astype(jnp.bfloat16)
        pltpu.make_async_copy(planes.at[block], near_out.at[block], out_sem.at[block]).start()
        return carry

    lax.fori_loop(0, MAXBLK, near_block, 0)

    for k in range(half, half + quarter):
        copies[k].wait_recv()

    for d in range(BAND):
        bands_to_lanes(ident, mid, d, first_q)

    def mid_block(block, carry):
        def table_row(s, row):
            return tab_mid[block, s, pl.ds(row, 1), :]

        sections_loop(first_q, buf_aq, buf_bq, stage_q, table_row, ident, True)
        planes_q[block] = stage_q[...].astype(jnp.bfloat16)
        pltpu.make_async_copy(planes_q.at[block], mid_out.at[block], out_sem_q.at[block]).start()
        return carry

    lax.fori_loop(0, MAXBLK, mid_block, 0)

    for block in range(MAXBLK):
        pltpu.make_async_copy(planes.at[block], near_out.at[block], out_sem.at[block]).wait()
        pltpu.make_async_copy(planes_q.at[block], mid_out.at[block], out_sem_q.at[block]).wait()
    tab_copy.wait()
    for k in range(1, n):
        copies[k].wait_send()
    for k in range(half + quarter, n):
        copies[k].wait_recv()


def turn(power, table, n):
    beams, chans, time_len = power.shape
    bands = chans // BAND
    sections, blocks, total_rows = table.shape
    half_rows = LANES * BAND
    tiles = time_len // TILE
    groups = total_rows // LANES
    any_spec = pl.BlockSpec(memory_space=pl.ANY)
    wide = pltpu.VMEM((BAND, tiles, TILE, LANES), jnp.float32)
    wide_q = pltpu.VMEM((BAND, tiles // 2, TILE, LANES), jnp.float32)
    ordered = (blocks, sections, BAND, LANES)
    return pl.pallas_call(
        functools.partial(turn_kernel, n, bands, time_len),
        out_shape=(
            jax.ShapeDtypeStruct((blocks, half_rows, time_len), jnp.bfloat16),
            jax.ShapeDtypeStruct((blocks, half_rows // 2, time_len), jnp.bfloat16),
            jax.ShapeDtypeStruct((n // 4, BAND, bands, time_len), jnp.bfloat16),
            jax.ShapeDtypeStruct(ordered, jnp.int32),
        ),
        in_specs=[any_spec, any_spec],
        out_specs=(any_spec, any_spec, any_spec, any_spec),
        scratch_shapes=[
            pltpu.VMEM((n, chans, time_len), jnp.bfloat16),
            pltpu.VMEM(table.shape, jnp.int32),
            pltpu.VMEM((chans, time_len), jnp.float32),
            pltpu.VMEM((n, BAND, bands, time_len), jnp.bfloat16),
            pltpu.VMEM((n // 2, BAND, bands, time_len), jnp.bfloat16),
            pltpu.VMEM((n // 4, BAND, bands, time_len), jnp.bfloat16),
            pltpu.VMEM((sections * blocks * groups, LANES), jnp.float32),
            pltpu.VMEM(ordered, jnp.int32),
            pltpu.VMEM(ordered, jnp.int32),
            pltpu.VMEM(ordered, jnp.int32),
            wide,
            wide,
            wide,
            pltpu.VMEM((half_rows, time_len), jnp.float32),
            wide_q,
            wide_q,
            wide_q,
            pltpu.VMEM((half_rows // 2, time_len), jnp.float32),
            pltpu.VMEM((blocks, half_rows, time_len), jnp.bfloat16),
            pltpu.VMEM((blocks, half_rows // 2, time_len), jnp.bfloat16),
            pltpu.SemaphoreType.DMA((n,)),
            pltpu.SemaphoreType.DMA,
            pltpu.SemaphoreType.DMA((n,)),
            pltpu.SemaphoreType.DMA((n,)),
            pltpu.SemaphoreType.DMA,
            pltpu.SemaphoreType.DMA((blocks,)),
            pltpu.SemaphoreType.DMA((blocks,)),
            pltpu.SemaphoreType.DMA,
        ],
        compiler_params=pltpu.CompilerParams(
            collective_id=0, has_side_effects=True, vmem_limit_bytes=58 * 2**20
        ),
        name="turn",
    )(power, table)


def fdmt_kernel(
    n, count_ref, far_hbm, tab_hbm, near_hbm, mid_hbm, o_hbm,
    x, tab, zeros, first, buf_a, buf_b, stage, done,
    in_sem, near_sem, mid_sem, zero_sem, done_sem,
):
    me = lax.axis_index("chan")
    count = count_ref[lax.axis_index("grp") * n + me]
    half = n // 2
    quarter = n // 4
    blocks, quarter_rows, _ = mid_hbm.shape

    def rows_of(first_quarter, size):
        start = pl.multiple_of(first_quarter * quarter_rows, quarter_rows)
        return pl.ds(start, size * quarter_rows)

    loads = [
        pltpu.make_async_copy(far_hbm, x, in_sem.at[0]),
        pltpu.make_async_copy(tab_hbm, tab, in_sem.at[1]),
    ]
    for load in loads:
        load.start()

    def near_copy(j):
        place = o_hbm.at[0, j, rows_of((me // half) * 2, 2)]
        return pltpu.make_async_copy(near_hbm.at[j], place, near_sem.at[j])

    def mid_copy(j):
        place = o_hbm.at[0, j, rows_of(flip(me, half) // quarter, 1)]
        return pltpu.make_async_copy(mid_hbm.at[j], place, mid_sem.at[j])

    def far_copy(j):
        place = o_hbm.at[0, j, rows_of(flip(me, half + quarter) // quarter, 1)]
        return pltpu.make_async_copy(done.at[j], place, done_sem.at[j])

    def zero_copy(j):
        return pltpu.make_async_copy(zeros, o_hbm.at[0, j], zero_sem.at[j])

    for j in range(blocks):

        @pl.when(j < count)
        def _(j=j):
            near_copy(j).start()
            mid_copy(j).start()

    @pl.when(count < blocks)
    def _():
        zeros[...] = jnp.zeros_like(zeros)

    for j in range(blocks):

        @pl.when(j >= count)
        def _(j=j):
            zero_copy(j).start()

    for load in loads:
        load.wait()
    ident = eye(LANES)
    for d in range(BAND):
        bands_to_lanes(ident, x, d, first)

    def far_block(j, carry):
        def table_row(s, row):
            return tab[j, s, pl.ds(row, 1), :]

        source = first
        for s in range(SECTIONS):
            target = (buf_a, buf_b)[s % 2]
            for p in range(BAND // 2):
                merge_pair(s, p, source, target, table_row, ident, stage, True)
            source = target
        done[j] = stage[...].astype(jnp.bfloat16)
        far_copy(j).start()
        return carry

    lax.fori_loop(0, count, far_block, 0)

    for j in range(blocks):

        @pl.when(j < count)
        def _(j=j):
            near_copy(j).wait()
            mid_copy(j).wait()
            far_copy(j).wait()

        @pl.when(j >= count)
        def _(j=j):
            zero_copy(j).wait()


def fdmt(counts, far, table, near, mid, n):
    time_len = far.shape[3]
    blocks, half_rows, _ = near.shape
    rows = 2 * half_rows
    quarter_rows = half_rows // 2
    wide = pltpu.VMEM((BAND, time_len // TILE // 2, TILE, LANES), jnp.float32)
    any_spec = pl.BlockSpec(memory_space=pl.ANY)
    return pl.pallas_call(
        functools.partial(fdmt_kernel, n),
        out_shape=jax.ShapeDtypeStruct((1, blocks, rows, time_len), jnp.bfloat16),
        in_specs=[pl.BlockSpec(memory_space=pltpu.SMEM)] + [any_spec] * 4,
        out_specs=any_spec,
        scratch_shapes=[
            pltpu.VMEM(far.shape, far.dtype),
            pltpu.VMEM(table.shape, table.dtype),
            pltpu.VMEM((rows, time_len), jnp.bfloat16),
            wide,
            wide,
            wide,
            pltpu.VMEM((quarter_rows, time_len), jnp.float32),
            pltpu.VMEM((blocks, quarter_rows, time_len), jnp.bfloat16),
            pltpu.SemaphoreType.DMA((2,)),
            pltpu.SemaphoreType.DMA((blocks,)),
            pltpu.SemaphoreType.DMA((blocks,)),
            pltpu.SemaphoreType.DMA((blocks,)),
            pltpu.SemaphoreType.DMA((blocks,)),
        ],
        compiler_params=pltpu.CompilerParams(vmem_limit_bytes=58 * 2**20),
        name="fdmt",
    )(counts, far, table, near, mid)


def body(beam_power, trial_blocks, shift_table):
    n = lax.axis_size("chan")
    near, mid, far, far_table = turn(beam_power, shift_table.swapaxes(0, 1), n)
    return fdmt(trial_blocks, far, far_table, near, mid, n)


def solution(mesh):
    in_specs = (P("grp", "chan", None), P(), P())
    out_specs = P(("grp", "chan"), None, None, None)
    return jax.shard_map(body, mesh=mesh, in_specs=in_specs, out_specs=out_specs, check_vma=False)
```

```python
import functools

import jax
import jax.numpy as jnp
from jax import lax
from jax.experimental import pallas as pl
from jax.experimental.pallas import tpu as pltpu
from jax.sharding import PartitionSpec as P

SECTIONS = 5
MAXBLK = 4
TILE = 8
BAND = 2**SECTIONS
LANES = 128
AT_ONCE = 4
MESH = pl.DeviceIdType.MESH

epsilon = 1e-05
out_scale = float(2**SECTIONS) ** (-0.5)


def flip(me, k):
    out = me
    bit = 1
    while bit <= k:
        if k & bit:
            out = out + bit * (1 - 2 * ((me // bit) % 2))
        bit *= 2
    return out


def eye(size):
    r = lax.broadcasted_iota(jnp.int32, (size, size), 0)
    c = lax.broadcasted_iota(jnp.int32, (size, size), 1)
    return (r == c).astype(jnp.float32).astype(jnp.bfloat16)


def times_transposed(a, b):
    return lax.dot_general(a, b, (((1,), (1,)), ((), ())), preferred_element_type=jnp.float32)


def bands_to_lanes(ident, x_ref, d, first):
    sources, _, bands, time_len = x_ref.shape
    if bands % 16 == 0:
        part = jnp.concatenate([x_ref[i, d] for i in range(sources)], axis=0)
    else:
        part = jnp.concatenate([x_ref[i, d].astype(jnp.float32) for i in range(sources)], axis=0)
        part = part.astype(jnp.bfloat16)
    turned = times_transposed(ident, part)
    if sources * bands < LANES:
        turned = jnp.concatenate([turned[: time_len // 2], turned[time_len // 2 :]], axis=1)
    first[d] = turned.reshape(first.shape[1:])


def merge_row(source, low_row, up_row, amount, split):
    tiles = source.shape[1]
    odd = (amount == 1) | (amount == 3)
    two = (amount == 2) | (amount == 3)
    four = amount == 4
    zero = jnp.zeros((TILE, LANES), jnp.float32)
    ups = {t: source[up_row, t] for t in range(tiles)}
    if split:
        late = lax.broadcasted_iota(jnp.int32, (TILE, LANES), 1) >= LANES // 2
        for t in range(-4, 0):
            ups[t] = jnp.where(late, pltpu.roll(ups[tiles + t], LANES // 2, 1), zero)
    ones, out = {}, []
    for t in range(-2 if split else 0, tiles):
        ones[t] = jnp.where(odd, ups.get(t - 1, zero), ups[t])
    for t in range(tiles):
        value = jnp.where(two, ones.get(t - 2, zero), ones[t])
        value = jnp.where(four, ups.get(t - 4, zero), value)
        out.append(source[low_row, t] + value)
    return out


def merge_pair(s, p, source, target, table_row, ident, stage, split):
    half = 2**s
    base = (p // half) * (2 * half)
    j = p % half
    if isinstance(p, int):
        after = min(j + 1, half - 1)
    else:
        after = jnp.minimum(j + 1, half - 1)
    rows = []
    for odd, up in ((0, j), (1, after)):
        amount = jnp.broadcast_to(table_row(s, 2 * p + odd), (TILE, LANES))
        rows.append(merge_row(source, base + j, base + half + up, amount, split))
    if s < SECTIONS - 1:
        for odd in range(2):
            for t, value in enumerate(rows[odd]):
                target[2 * p + odd, t] = value
        return
    time_len = len(rows[0]) * TILE
    both = [(value * out_scale) for row in rows for value in row]
    both = jnp.concatenate(both, axis=0).astype(jnp.bfloat16)
    turned = times_transposed(ident, both)
    bands = LANES // 2 if split else LANES
    for odd in range(2):
        row = turned[:, odd * time_len : (odd + 1) * time_len]
        if split:
            row = jnp.concatenate([row[:bands], row[bands:]], axis=1)
        stage[pl.ds(2 * p + odd, bands, stride=BAND), :] = row


def sections_loop(first, buf_a, buf_b, stage, table_row, ident, split):
    source = first
    for s in range(SECTIONS):
        target = (buf_a, buf_b)[s % 2]

        def step(i, inner, s=s, source=source, target=target):
            for p in range(AT_ONCE):
                merge_pair(s, i * AT_ONCE + p, source, target, table_row, ident, stage, split)
            return inner

        lax.fori_loop(0, BAND // 2 // AT_ONCE, step, 0)
        source = target


def turn_kernel(
    n, bands, time_len,
    power_hbm, table_hbm,
    near_out, mid_out, far_ref, far_table,
    power, table, rows, packed, near, mid, lines, tab_near, tab_mid, tab_far,
    first, buf_a, buf_b, stage, first_q, buf_aq, buf_bq, stage_q, planes, planes_q,
    in_sem, table_sem, send_sem, recv_sem, own_sem, out_sem, out_sem_q, tab_sem,
):
    me = lax.axis_index("chan")
    grp = lax.axis_index("grp")
    half = n // 2
    quarter = n // 4
    near_ks = list(range(half - 1, -1, -1))
    mid_ks = list(range(half, half + quarter))
    far_ks = list(range(half + quarter, n))

    loads = {}
    for i in range(half):
        for k in near_ks[i : i + 1] + mid_ks[i : i + 1]:
            loads[k] = pltpu.make_async_copy(power_hbm.at[flip(me, k)], power.at[k], in_sem.at[k])
            loads[k].start()
    for k in far_ks:
        loads[k] = pltpu.make_async_copy(power_hbm.at[flip(me, k)], power.at[k], in_sem.at[k])
        loads[k].start()
    table_load = pltpu.make_async_copy(table_hbm, table, table_sem)
    table_load.start()

    barrier = pltpu.get_barrier_semaphore()
    for k in range(1, n):
        pl.semaphore_signal(barrier, inc=1, device_id=(flip(me, k), grp), device_id_type=MESH)
    pl.semaphore_wait(barrier, n - 1)

    copies = {}
    for k in range(n):
        if k < half:
            place = near.at[me % half]
        elif k < half + quarter:
            place = mid.at[me % quarter]
        else:
            place = far_ref.at[me % quarter]
        if k == 0:
            copies[k] = pltpu.make_async_copy(packed.at[k], place, own_sem)
        else:
            copies[k] = pltpu.make_async_remote_copy(
                src_ref=packed.at[k],
                dst_ref=place,
                send_sem=send_sem.at[k],
                recv_sem=recv_sem.at[k],
                device_id=(flip(me, k), grp),
                device_id_type=MESH,
            )

    def send(ks):
        for k in ks:
            loads[k].wait()
            values = power[k].astype(jnp.float32)
            center = jnp.mean(values, axis=-1, keepdims=True)
            moved = values - center
            spread = jnp.mean(jnp.square(moved), axis=-1, keepdims=True)
            rows[...] = moved * lax.rsqrt(spread + epsilon)
            for d in range(BAND):
                packed[k, d] = rows[pl.ds(d, bands, stride=BAND), :].astype(jnp.bfloat16)
            copies[k].start()

    @pl.when(grp % 2 == 0)
    def _():
        send(near_ks + mid_ks)

    @pl.when(grp % 2 != 0)
    def _():
        send(mid_ks + near_ks)

    send(far_ks)

    table_load.wait()
    ident = eye(LANES)
    groups = table.shape[2] // LANES
    per_group = LANES // BAND
    pairs = SECTIONS * MAXBLK // 2

    def spread_table(s, carry):
        for c in range(groups):
            lines[pl.ds(s * (MAXBLK * groups) + c, MAXBLK, stride=groups), :] = table[
                s, :, c * LANES : (c + 1) * LANES
            ].astype(jnp.float32)
        return carry

    lax.fori_loop(0, SECTIONS, spread_table, 0)
    turned = times_transposed(ident, lines[...].astype(jnp.bfloat16))
    turned = jnp.concatenate(
        [
            jnp.concatenate(
                [
                    turned[b * BAND : (b + 1) * BAND, q * 2 * groups : (q + 1) * 2 * groups]
                    for b in range(per_group)
                ],
                axis=1,
            )
            for q in range(pairs)
        ],
        axis=0,
    ).astype(jnp.bfloat16)
    shape = (per_group * 2 * groups, 2 * LANES)
    index = lax.broadcasted_iota(jnp.int32, shape, 0)
    lane = lax.broadcasted_iota(jnp.int32, shape, 1)
    same = (index // groups) % 2 == lane // LANES
    band = (index % groups) * per_group + index // (2 * groups)
    parts = (
        ((me // half) * LANES, lane % LANES, tab_near),
        ((flip(me, half) // quarter) * (LANES // 2), lane % (LANES // 2), tab_mid),
        ((flip(me, half + quarter) // quarter) * (LANES // 2), lane % (LANES // 2), tab_far),
    )
    for start, lanes, target in parts:
        place = (same & (band - start == lanes)).astype(jnp.float32).astype(jnp.bfloat16)
        placed = jnp.dot(turned, place, preferred_element_type=jnp.float32).astype(jnp.int32)
        for q in range(pairs):
            for i in range(2):
                s, block = divmod(2 * q + i, MAXBLK)
                target[block, s] = placed[q * BAND : (q + 1) * BAND, i * LANES : (i + 1) * LANES]
    tab_copy = pltpu.make_async_copy(tab_far, far_table, tab_sem)
    tab_copy.start()

    copies[0].wait()
    for k in range(1, half):
        copies[k].wait_recv()

    for d in range(BAND):
        bands_to_lanes(ident, near, d, first)

    def near_block(block, carry):
        def table_row(s, row):
            return tab_near[block, s, pl.ds(row, 1), :]

        sections_loop(first, buf_a, buf_b, stage, table_row, ident, False)
        planes[block] = stage[...].astype(jnp.bfloat16)
        pltpu.make_async_copy(planes.at[block], near_out.at[block], out_sem.at[block]).start()
        return carry

    lax.fori_loop(0, MAXBLK, near_block, 0)

    for k in range(half, half + quarter):
        copies[k].wait_recv()

    for d in range(BAND):
        bands_to_lanes(ident, mid, d, first_q)

    def mid_block(block, carry):
        def table_row(s, row):
            return tab_mid[block, s, pl.ds(row, 1), :]

        sections_loop(first_q, buf_aq, buf_bq, stage_q, table_row, ident, True)
        planes_q[block] = stage_q[...].astype(jnp.bfloat16)
        pltpu.make_async_copy(planes_q.at[block], mid_out.at[block], out_sem_q.at[block]).start()
        return carry

    lax.fori_loop(0, MAXBLK, mid_block, 0)

    for block in range(MAXBLK):
        pltpu.make_async_copy(planes.at[block], near_out.at[block], out_sem.at[block]).wait()
        pltpu.make_async_copy(planes_q.at[block], mid_out.at[block], out_sem_q.at[block]).wait()
    tab_copy.wait()
    for k in range(1, n):
        copies[k].wait_send()
    for k in range(half + quarter, n):
        copies[k].wait_recv()


def turn(power, table, n):
    beams, chans, time_len = power.shape
    bands = chans // BAND
    sections, blocks, total_rows = table.shape
    half_rows = LANES * BAND
    tiles = time_len // TILE
    groups = total_rows // LANES
    any_spec = pl.BlockSpec(memory_space=pl.ANY)
    wide = pltpu.VMEM((BAND, tiles, TILE, LANES), jnp.float32)
    wide_q = pltpu.VMEM((BAND, tiles // 2, TILE, LANES), jnp.float32)
    ordered = (blocks, sections, BAND, LANES)
    return pl.pallas_call(
        functools.partial(turn_kernel, n, bands, time_len),
        out_shape=(
            jax.ShapeDtypeStruct((blocks, half_rows, time_len), jnp.bfloat16),
            jax.ShapeDtypeStruct((blocks, half_rows // 2, time_len), jnp.bfloat16),
            jax.ShapeDtypeStruct((n // 4, BAND, bands, time_len), jnp.bfloat16),
            jax.ShapeDtypeStruct(ordered, jnp.int32),
        ),
        in_specs=[any_spec, any_spec],
        out_specs=(any_spec, any_spec, any_spec, any_spec),
        scratch_shapes=[
            pltpu.VMEM((n, chans, time_len), jnp.bfloat16),
            pltpu.VMEM(table.shape, jnp.int32),
            pltpu.VMEM((chans, time_len), jnp.float32),
            pltpu.VMEM((n, BAND, bands, time_len), jnp.bfloat16),
            pltpu.VMEM((n // 2, BAND, bands, time_len), jnp.bfloat16),
            pltpu.VMEM((n // 4, BAND, bands, time_len), jnp.bfloat16),
            pltpu.VMEM((sections * blocks * groups, LANES), jnp.float32),
            pltpu.VMEM(ordered, jnp.int32),
            pltpu.VMEM(ordered, jnp.int32),
            pltpu.VMEM(ordered, jnp.int32),
            wide,
            wide,
            wide,
            pltpu.VMEM((half_rows, time_len), jnp.float32),
            wide_q,
            wide_q,
            wide_q,
            pltpu.VMEM((half_rows // 2, time_len), jnp.float32),
            pltpu.VMEM((blocks, half_rows, time_len), jnp.bfloat16),
            pltpu.VMEM((blocks, half_rows // 2, time_len), jnp.bfloat16),
            pltpu.SemaphoreType.DMA((n,)),
            pltpu.SemaphoreType.DMA,
            pltpu.SemaphoreType.DMA((n,)),
            pltpu.SemaphoreType.DMA((n,)),
            pltpu.SemaphoreType.DMA,
            pltpu.SemaphoreType.DMA((blocks,)),
            pltpu.SemaphoreType.DMA((blocks,)),
            pltpu.SemaphoreType.DMA,
        ],
        compiler_params=pltpu.CompilerParams(
            collective_id=0, has_side_effects=True, vmem_limit_bytes=58 * 2**20
        ),
        name="turn",
    )(power, table)


def fdmt_kernel(
    n, count_ref, far_hbm, tab_hbm, near_hbm, mid_hbm, o_hbm,
    x, tab, zeros, near, mid, first, buf_a, buf_b, stage, done,
    in_sem, near_in, mid_in, near_sem, mid_sem, zero_sem, done_sem,
):
    me = lax.axis_index("chan")
    count = count_ref[lax.axis_index("grp") * n + me]
    half = n // 2
    quarter = n // 4
    blocks, quarter_rows, _ = mid_hbm.shape

    def rows_of(first_quarter, size):
        start = pl.multiple_of(first_quarter * quarter_rows, quarter_rows)
        return pl.ds(start, size * quarter_rows)

    loads = [
        pltpu.make_async_copy(far_hbm, x, in_sem.at[0]),
        pltpu.make_async_copy(tab_hbm, tab, in_sem.at[1]),
    ]
    for load in loads:
        load.start()

    def near_copy(j):
        place = o_hbm.at[0, j, rows_of((me // half) * 2, 2)]
        return pltpu.make_async_copy(near.at[j], place, near_sem.at[j])

    def mid_copy(j):
        place = o_hbm.at[0, j, rows_of(flip(me, half) // quarter, 1)]
        return pltpu.make_async_copy(mid.at[j], place, mid_sem.at[j])

    def far_copy(j):
        place = o_hbm.at[0, j, rows_of(flip(me, half + quarter) // quarter, 1)]
        return pltpu.make_async_copy(done.at[j], place, done_sem.at[j])

    def zero_copy(j):
        return pltpu.make_async_copy(zeros, o_hbm.at[0, j], zero_sem.at[j])

    def near_load(j):
        return pltpu.make_async_copy(near_hbm.at[j], near.at[j], near_in.at[j])

    def mid_load(j):
        return pltpu.make_async_copy(mid_hbm.at[j], mid.at[j], mid_in.at[j])

    for j in range(blocks):

        @pl.when(j < count)
        def _(j=j):
            near_load(j).start()
            mid_load(j).start()

    @pl.when(count < blocks)
    def _():
        zeros[...] = jnp.zeros_like(zeros)

    for j in range(blocks):

        @pl.when(j >= count)
        def _(j=j):
            zero_copy(j).start()

    for load in loads:
        load.wait()
    ident = eye(LANES)
    for d in range(BAND):
        bands_to_lanes(ident, x, d, first)

    for j in range(blocks):

        @pl.when(j < count)
        def _(j=j):
            near_load(j).wait()
            near_copy(j).start()
            mid_load(j).wait()
            mid_copy(j).start()

    def far_block(j, carry):
        def table_row(s, row):
            return tab[j, s, pl.ds(row, 1), :]

        source = first
        for s in range(SECTIONS):
            target = (buf_a, buf_b)[s % 2]
            for p in range(BAND // 2):
                merge_pair(s, p, source, target, table_row, ident, stage, True)
            source = target
        done[j] = stage[...].astype(jnp.bfloat16)
        far_copy(j).start()
        return carry

    lax.fori_loop(0, count, far_block, 0)

    for j in range(blocks):

        @pl.when(j < count)
        def _(j=j):
            near_copy(j).wait()
            mid_copy(j).wait()
            far_copy(j).wait()

        @pl.when(j >= count)
        def _(j=j):
            zero_copy(j).wait()


def fdmt(counts, far, table, near, mid, n):
    time_len = far.shape[3]
    blocks, half_rows, _ = near.shape
    rows = 2 * half_rows
    quarter_rows = half_rows // 2
    wide = pltpu.VMEM((BAND, time_len // TILE // 2, TILE, LANES), jnp.float32)
    any_spec = pl.BlockSpec(memory_space=pl.ANY)
    return pl.pallas_call(
        functools.partial(fdmt_kernel, n),
        out_shape=jax.ShapeDtypeStruct((1, blocks, rows, time_len), jnp.bfloat16),
        in_specs=[pl.BlockSpec(memory_space=pltpu.SMEM)] + [any_spec] * 4,
        out_specs=any_spec,
        scratch_shapes=[
            pltpu.VMEM(far.shape, far.dtype),
            pltpu.VMEM(table.shape, table.dtype),
            pltpu.VMEM((rows, time_len), jnp.bfloat16),
            pltpu.VMEM(near.shape, near.dtype),
            pltpu.VMEM(mid.shape, mid.dtype),
            wide,
            wide,
            wide,
            pltpu.VMEM((quarter_rows, time_len), jnp.float32),
            pltpu.VMEM((blocks, quarter_rows, time_len), jnp.bfloat16),
            pltpu.SemaphoreType.DMA((2,)),
            pltpu.SemaphoreType.DMA((blocks,)),
            pltpu.SemaphoreType.DMA((blocks,)),
            pltpu.SemaphoreType.DMA((blocks,)),
            pltpu.SemaphoreType.DMA((blocks,)),
            pltpu.SemaphoreType.DMA((blocks,)),
            pltpu.SemaphoreType.DMA((blocks,)),
        ],
        compiler_params=pltpu.CompilerParams(vmem_limit_bytes=58 * 2**20),
        name="fdmt",
    )(counts, far, table, near, mid)


def body(beam_power, trial_blocks, shift_table):
    n = lax.axis_size("chan")
    near, mid, far, far_table = turn(beam_power, shift_table.swapaxes(0, 1), n)
    return fdmt(trial_blocks, far, far_table, near, mid, n)


def solution(mesh):
    in_specs = (P("grp", "chan", None), P(), P())
    out_specs = P(("grp", "chan"), None, None, None)
    return jax.shard_map(body, mesh=mesh, in_specs=in_specs, out_specs=out_specs, check_vma=False)
```

```python
import functools

import jax
import jax.numpy as jnp
from jax import lax
from jax.experimental import pallas as pl
from jax.experimental.pallas import tpu as pltpu
from jax.sharding import PartitionSpec as P

SECTIONS = 5
MAXBLK = 4
TILE = 8
BAND = 2**SECTIONS
LANES = 128
AT_ONCE = 4
MESH = pl.DeviceIdType.MESH

epsilon = 1e-05
out_scale = float(2**SECTIONS) ** (-0.5)


def flip(me, k):
    out = me
    bit = 1
    while bit <= k:
        if k & bit:
            out = out + bit * (1 - 2 * ((me // bit) % 2))
        bit *= 2
    return out


def eye(size):
    r = lax.broadcasted_iota(jnp.int32, (size, size), 0)
    c = lax.broadcasted_iota(jnp.int32, (size, size), 1)
    return (r == c).astype(jnp.float32).astype(jnp.bfloat16)


def times_transposed(a, b):
    return lax.dot_general(a, b, (((1,), (1,)), ((), ())), preferred_element_type=jnp.float32)


def bands_to_lanes(ident, x_ref, d, first):
    sources, _, bands, time_len = x_ref.shape
    if bands % 16 == 0:
        part = jnp.concatenate([x_ref[i, d] for i in range(sources)], axis=0)
    else:
        part = jnp.concatenate([x_ref[i, d].astype(jnp.float32) for i in range(sources)], axis=0)
        part = part.astype(jnp.bfloat16)
    turned = times_transposed(ident, part)
    if sources * bands < LANES:
        turned = jnp.concatenate([turned[: time_len // 2], turned[time_len // 2 :]], axis=1)
    first[d] = turned.reshape(first.shape[1:])


def merge_row(source, low_row, up_row, amount, split):
    tiles = source.shape[1]
    odd = (amount == 1) | (amount == 3)
    two = (amount == 2) | (amount == 3)
    four = amount == 4
    zero = jnp.zeros((TILE, LANES), jnp.float32)
    ups = {t: source[up_row, t] for t in range(tiles)}
    if split:
        late = lax.broadcasted_iota(jnp.int32, (TILE, LANES), 1) >= LANES // 2
        for t in range(-4, 0):
            ups[t] = jnp.where(late, pltpu.roll(ups[tiles + t], LANES // 2, 1), zero)
    ones, out = {}, []
    for t in range(-2 if split else 0, tiles):
        ones[t] = jnp.where(odd, ups.get(t - 1, zero), ups[t])
    for t in range(tiles):
        value = jnp.where(two, ones.get(t - 2, zero), ones[t])
        value = jnp.where(four, ups.get(t - 4, zero), value)
        out.append(source[low_row, t] + value)
    return out


def merge_pair(s, p, source, target, table_row, ident, stage, split):
    half = 2**s
    base = (p // half) * (2 * half)
    j = p % half
    if isinstance(p, int):
        after = min(j + 1, half - 1)
    else:
        after = jnp.minimum(j + 1, half - 1)
    rows = []
    for odd, up in ((0, j), (1, after)):
        amount = jnp.broadcast_to(table_row(s, 2 * p + odd), (TILE, LANES))
        rows.append(merge_row(source, base + j, base + half + up, amount, split))
    if s < SECTIONS - 1:
        for odd in range(2):
            for t, value in enumerate(rows[odd]):
                target[2 * p + odd, t] = value
        return
    time_len = len(rows[0]) * TILE
    both = [(value * out_scale) for row in rows for value in row]
    both = jnp.concatenate(both, axis=0).astype(jnp.bfloat16)
    turned = times_transposed(ident, both)
    bands = LANES // 2 if split else LANES
    for odd in range(2):
        row = turned[:, odd * time_len : (odd + 1) * time_len]
        if split:
            row = jnp.concatenate([row[:bands], row[bands:]], axis=1)
        stage[pl.ds(2 * p + odd, bands, stride=BAND), :] = row


def sections_loop(first, buf_a, buf_b, stage, table_row, ident, split):
    source = first
    for s in range(SECTIONS):
        target = (buf_a, buf_b)[s % 2]

        def step(i, inner, s=s, source=source, target=target):
            for p in range(AT_ONCE):
                merge_pair(s, i * AT_ONCE + p, source, target, table_row, ident, stage, split)
            return inner

        lax.fori_loop(0, BAND // 2 // AT_ONCE, step, 0)
        source = target


def turn_kernel(
    n, bands, time_len,
    power_hbm, table_hbm,
    near_out, mid_out, far_ref, far_table,
    power, table, rows, packed, near, mid, lines, tab_near, tab_mid, tab_far,
    first, buf_a, buf_b, stage, first_q, buf_aq, buf_bq, stage_q, planes, planes_q,
    in_sem, table_sem, send_sem, recv_sem, own_sem, out_sem, out_sem_q, tab_sem,
):
    me = lax.axis_index("chan")
    grp = lax.axis_index("grp")
    half = n // 2
    quarter = n // 4
    order = list(range(half - 1, -1, -1)) + list(range(half, n))

    loads = {}
    for k in order:
        loads[k] = pltpu.make_async_copy(power_hbm.at[flip(me, k)], power.at[k], in_sem.at[k])
        loads[k].start()
    table_load = pltpu.make_async_copy(table_hbm, table, table_sem)
    table_load.start()

    barrier = pltpu.get_barrier_semaphore()
    for k in range(1, n):
        pl.semaphore_signal(barrier, inc=1, device_id=(flip(me, k), grp), device_id_type=MESH)
    pl.semaphore_wait(barrier, n - 1)

    copies = {}
    for k in order:
        loads[k].wait()
        values = power[k].astype(jnp.float32)
        center = jnp.mean(values, axis=-1, keepdims=True)
        moved = values - center
        spread = jnp.mean(jnp.square(moved), axis=-1, keepdims=True)
        rows[...] = moved * lax.rsqrt(spread + epsilon)
        for d in range(BAND):
            packed[k, d] = rows[pl.ds(d, bands, stride=BAND), :].astype(jnp.bfloat16)
        if k < half:
            place = near.at[me % half]
        elif k < half + quarter:
            place = mid.at[me % quarter]
        else:
            place = far_ref.at[me % quarter]
        if k == 0:
            copies[k] = pltpu.make_async_copy(packed.at[k], place, own_sem)
        else:
            copies[k] = pltpu.make_async_remote_copy(
                src_ref=packed.at[k],
                dst_ref=place,
                send_sem=send_sem.at[k],
                recv_sem=recv_sem.at[k],
                device_id=(flip(me, k), grp),
                device_id_type=MESH,
            )
        copies[k].start()

    table_load.wait()
    ident = eye(LANES)
    groups = table.shape[2] // LANES
    per_group = LANES // BAND
    pairs = SECTIONS * MAXBLK // 2

    def spread_table(s, carry):
        for c in range(groups):
            lines[pl.ds(s * (MAXBLK * groups) + c, MAXBLK, stride=groups), :] = table[
                s, :, c * LANES : (c + 1) * LANES
            ].astype(jnp.float32)
        return carry

    lax.fori_loop(0, SECTIONS, spread_table, 0)
    turned = times_transposed(ident, lines[...].astype(jnp.bfloat16))
    turned = jnp.concatenate(
        [
            jnp.concatenate(
                [
                    turned[b * BAND : (b + 1) * BAND, q * 2 * groups : (q + 1) * 2 * groups]
                    for b in range(per_group)
                ],
                axis=1,
            )
            for q in range(pairs)
        ],
        axis=0,
    ).astype(jnp.bfloat16)
    shape = (per_group * 2 * groups, 2 * LANES)
    index = lax.broadcasted_iota(jnp.int32, shape, 0)
    lane = lax.broadcasted_iota(jnp.int32, shape, 1)
    same = (index // groups) % 2 == lane // LANES
    band = (index % groups) * per_group + index // (2 * groups)
    parts = (
        ((me // half) * LANES, lane % LANES, tab_near),
        ((flip(me, half) // quarter) * (LANES // 2), lane % (LANES // 2), tab_mid),
        ((flip(me, half + quarter) // quarter) * (LANES // 2), lane % (LANES // 2), tab_far),
    )
    for start, lanes, target in parts:
        place = (same & (band - start == lanes)).astype(jnp.float32).astype(jnp.bfloat16)
        placed = jnp.dot(turned, place, preferred_element_type=jnp.float32).astype(jnp.int32)
        for q in range(pairs):
            for i in range(2):
                s, block = divmod(2 * q + i, MAXBLK)
                target[block, s] = placed[q * BAND : (q + 1) * BAND, i * LANES : (i + 1) * LANES]
    tab_copy = pltpu.make_async_copy(tab_far, far_table, tab_sem)
    tab_copy.start()

    copies[0].wait()
    for k in range(1, half):
        copies[k].wait_recv()

    for d in range(BAND):
        bands_to_lanes(ident, near, d, first)

    def near_block(block, carry):
        def table_row(s, row):
            return tab_near[block, s, pl.ds(row, 1), :]

        sections_loop(first, buf_a, buf_b, stage, table_row, ident, False)
        planes[block] = stage[...].astype(jnp.bfloat16)
        pltpu.make_async_copy(planes.at[block], near_out.at[block], out_sem.at[block]).start()
        return carry

    lax.fori_loop(0, MAXBLK, near_block, 0)

    for k in range(half, half + quarter):
        copies[k].wait_recv()

    for d in range(BAND):
        bands_to_lanes(ident, mid, d, first_q)

    def mid_block(block, carry):
        def table_row(s, row):
            return tab_mid[block, s, pl.ds(row, 1), :]

        sections_loop(first_q, buf_aq, buf_bq, stage_q, table_row, ident, True)
        planes_q[block] = stage_q[...].astype(jnp.bfloat16)
        pltpu.make_async_copy(planes_q.at[block], mid_out.at[block], out_sem_q.at[block]).start()
        return carry

    lax.fori_loop(0, MAXBLK, mid_block, 0)

    for block in range(MAXBLK):
        pltpu.make_async_copy(planes.at[block], near_out.at[block], out_sem.at[block]).wait()
        pltpu.make_async_copy(planes_q.at[block], mid_out.at[block], out_sem_q.at[block]).wait()
    tab_copy.wait()
    for k in range(1, n):
        copies[k].wait_send()
    for k in range(half + quarter, n):
        copies[k].wait_recv()


def turn(power, table, n):
    beams, chans, time_len = power.shape
    bands = chans // BAND
    sections, blocks, total_rows = table.shape
    half_rows = LANES * BAND
    tiles = time_len // TILE
    groups = total_rows // LANES
    any_spec = pl.BlockSpec(memory_space=pl.ANY)
    wide = pltpu.VMEM((BAND, tiles, TILE, LANES), jnp.float32)
    wide_q = pltpu.VMEM((BAND, tiles // 2, TILE, LANES), jnp.float32)
    ordered = (blocks, sections, BAND, LANES)
    return pl.pallas_call(
        functools.partial(turn_kernel, n, bands, time_len),
        out_shape=(
            jax.ShapeDtypeStruct((blocks, half_rows, time_len), jnp.bfloat16),
            jax.ShapeDtypeStruct((blocks, half_rows // 2, time_len), jnp.bfloat16),
            jax.ShapeDtypeStruct((n // 4, BAND, bands, time_len), jnp.bfloat16),
            jax.ShapeDtypeStruct(ordered, jnp.int32),
        ),
        in_specs=[any_spec, any_spec],
        out_specs=(any_spec, any_spec, any_spec, any_spec),
        scratch_shapes=[
            pltpu.VMEM((n, chans, time_len), jnp.bfloat16),
            pltpu.VMEM(table.shape, jnp.int32),
            pltpu.VMEM((chans, time_len), jnp.float32),
            pltpu.VMEM((n, BAND, bands, time_len), jnp.bfloat16),
            pltpu.VMEM((n // 2, BAND, bands, time_len), jnp.bfloat16),
            pltpu.VMEM((n // 4, BAND, bands, time_len), jnp.bfloat16),
            pltpu.VMEM((sections * blocks * groups, LANES), jnp.float32),
            pltpu.VMEM(ordered, jnp.int32),
            pltpu.VMEM(ordered, jnp.int32),
            pltpu.VMEM(ordered, jnp.int32),
            wide,
            wide,
            wide,
            pltpu.VMEM((half_rows, time_len), jnp.float32),
            wide_q,
            wide_q,
            wide_q,
            pltpu.VMEM((half_rows // 2, time_len), jnp.float32),
            pltpu.VMEM((blocks, half_rows, time_len), jnp.bfloat16),
            pltpu.VMEM((blocks, half_rows // 2, time_len), jnp.bfloat16),
            pltpu.SemaphoreType.DMA((n,)),
            pltpu.SemaphoreType.DMA,
            pltpu.SemaphoreType.DMA((n,)),
            pltpu.SemaphoreType.DMA((n,)),
            pltpu.SemaphoreType.DMA,
            pltpu.SemaphoreType.DMA((blocks,)),
            pltpu.SemaphoreType.DMA((blocks,)),
            pltpu.SemaphoreType.DMA,
        ],
        compiler_params=pltpu.CompilerParams(
            collective_id=0, has_side_effects=True, vmem_limit_bytes=58 * 2**20
        ),
        name="turn",
    )(power, table)


def fdmt_kernel(n, count_ref, x_ref, tab_ref, near_ref, mid_ref, o_ref, first, buf_a, buf_b, stage):
    block = pl.program_id(0)
    me = lax.axis_index("chan")
    count = count_ref[lax.axis_index("grp") * n + me]
    half = n // 2
    quarter = n // 4
    quarter_rows = mid_ref.shape[1]

    def rows_of(first_quarter, size):
        start = pl.multiple_of(first_quarter * quarter_rows, quarter_rows)
        return pl.ds(start, size * quarter_rows)

    @pl.when(block == 0)
    def _():
        ident = eye(x_ref.shape[3])
        for d in range(BAND):
            bands_to_lanes(ident, x_ref, d, first)

    @pl.when(block < count)
    def _():
        ident = eye(LANES)

        def table_row(s, row):
            return tab_ref[0, s, pl.ds(row, 1), :]

        o_ref[0, 0, rows_of((me // half) * 2, 2), :] = near_ref[0]
        o_ref[0, 0, rows_of(flip(me, half) // quarter, 1), :] = mid_ref[0]
        source = first
        for s in range(SECTIONS):
            target = (buf_a, buf_b)[s % 2]
            for p in range(BAND // 2):
                merge_pair(s, p, source, target, table_row, ident, stage, True)
            source = target
        o_ref[0, 0, rows_of(flip(me, half + quarter) // quarter, 1), :] = stage[...].astype(jnp.bfloat16)

    @pl.when(block >= count)
    def _():
        o_ref[...] = jnp.zeros_like(o_ref)


def fdmt(counts, far, table, near, mid, n):
    sources, _, bands, time_len = far.shape
    blocks, half_rows, _ = near.shape
    rows = 2 * half_rows
    wide = pltpu.VMEM((BAND, time_len // TILE // 2, TILE, LANES), jnp.float32)
    return pl.pallas_call(
        functools.partial(fdmt_kernel, n),
        grid=(blocks,),
        out_shape=jax.ShapeDtypeStruct((1, blocks, rows, time_len), jnp.bfloat16),
        in_specs=[
            pl.BlockSpec(memory_space=pltpu.SMEM),
            pl.BlockSpec(far.shape, lambda j: (0, 0, 0, 0)),
            pl.BlockSpec((1,) + table.shape[1:], lambda j: (j, 0, 0, 0)),
            pl.BlockSpec((1, half_rows, time_len), lambda j: (j, 0, 0)),
            pl.BlockSpec((1, half_rows // 2, time_len), lambda j: (j, 0, 0)),
        ],
        out_specs=pl.BlockSpec((1, 1, rows, time_len), lambda j: (0, j, 0, 0)),
        scratch_shapes=[wide, wide, wide, pltpu.VMEM((half_rows // 2, time_len), jnp.float32)],
        compiler_params=pltpu.CompilerParams(vmem_limit_bytes=58 * 2**20),
        name="fdmt",
    )(counts, far, table, near, mid)


def body(beam_power, trial_blocks, shift_table):
    n = lax.axis_size("chan")
    near, mid, far, far_table = turn(beam_power, shift_table.swapaxes(0, 1), n)
    return fdmt(trial_blocks, far, far_table, near, mid, n)


def solution(mesh):
    in_specs = (P("grp", "chan", None), P(), P())
    out_specs = P(("grp", "chan"), None, None, None)
    return jax.shard_map(body, mesh=mesh, in_specs=in_specs, out_specs=out_specs, check_vma=False)
```
